256 devices in a mesh: layer: 32 (over y, z), feat: 8 (over x, core).
Axes of the slice: x: 4, y: 4, z: 8, core: 2. Of those that a mesh axis runs over, the one named last changes fastest.
Arguments:
- encoder: bfloat16 [32, 2304, 8192], P('layer', None, 'feat'), may hold values from -0.125 to 0.125
- decoder: bfloat16 [32, 8192, 2304], P('layer', 'feat'), may hold values from -1 to 1
- chosen: int32 [128], replicated, may hold values from 0 to 8191
Outputs:
- virtual: bfloat16 [32, 128, 8192], P('layer', None, 'feat')
The draws below stay inside these ranges and needn't reach their ends.
Inputs may be any that keep to these rules, and one draw needn't show every extreme that they name: `chosen`: each index names one of the source layer's 8192 features.
All inputs are finite; a program needn't handle non-finite values.
Results may differ from the reference program's by a relative error of at most 0.015.
Values may be sent and summed in bfloat16 or wider, within the bound.
No kernel may reach another device: no remote copies, remote signals or barrier semaphores. Data moves between devices by JAX's collectives and lax.ppermute only.
A program may use at most 128 MiB of HBM per device.

```python
import jax
import jax.numpy as jnp
from jax import lax

D = 2304
F = 8192
K = 128
L = 32


def set_ends(array, own_key, least, high):
    extent = array.shape
    spot = [jax.random.randint(jax.random.fold_in(own_key, axis), (), 0, extent[axis]) for axis in range(len(extent))]
    array = array.at[tuple(spot)].set(least)
    longest = extent.index(max(extent))
    spot[longest] = (spot[longest] + 1) % extent[longest]
    return array.at[tuple(spot)].set(high)


def block_levels(stream_key, extent, split, low, high):
    loudness, own = 1.0, jax.random.fold_in(stream_key, 6)
    for dim, shards_of in split:
        heights = jnp.exp(jax.random.uniform(jax.random.fold_in(own, dim), (shards_of,), jnp.float32, low / len(split), high / len(split)))
        loudness = loudness * jnp.repeat(heights, extent[dim] // shards_of).reshape([-1 if axis == dim else 1 for axis in range(len(extent))])
    return loudness


def noise(key, dims, scale, limit, pieces=(), dtype=jnp.bfloat16):
    drawn = jax.random.normal(key, dims, jnp.float32) * scale
    if len(pieces) > 0:
        drawn = block_levels(key, dims, pieces, -0.22, 0.18) * drawn
    return jnp.clip(drawn, min=-limit, max=limit).astype(dtype)


def setup_inputs(seed: int = 0) -> dict:
    keys = jax.random.split(jax.random.key(seed), 4)
    encoder = noise(keys[0], (L, D, F), D ** -0.5, 0.125, ((0, 32), (2, 8)))
    decoder = noise(keys[1], (L, F, D), L ** -0.5, 1.0, ((0, 32), (1, 8)))
    chosen = set_ends(jax.random.randint(keys[2], (K,), 0, F), jax.random.fold_in(keys[2], 1), 0, F - 1).astype(jnp.int32)
    return {"encoder": encoder, "decoder": decoder, "chosen": chosen}


def reference(encoder, decoder, chosen):
    rows = jnp.take(decoder, chosen, axis=1)
    terms = rows.astype(jnp.float32)
    zeros = jnp.zeros((1, K, D), jnp.float32)
    prefix = jnp.concatenate([zeros, jnp.cumsum(terms[:-1], axis=0)], axis=0)
    prefix_low = prefix.astype(jnp.bfloat16)

    def product(pair):
        return jnp.dot(pair[0], pair[1], preferred_element_type=jnp.float32).astype(jnp.bfloat16)

    return lax.map(product, (prefix_low, encoder))
```

```python
import jax
import jax.numpy as jnp
from jax import lax
from jax.sharding import PartitionSpec as P

BF = jnp.bfloat16
F32 = jnp.float32


def local(encoder, decoder, chosen):
    enc, dec = encoder[0], decoder[0]
    feats, width = dec.shape
    k = chosen.shape[0]
    half, rows = width // 2, k // 4
    feat, layer = lax.axis_index("feat"), lax.axis_index("layer")
    x, c = feat // 2, feat % 2
    z = layer % 8

    def feat_step(v, move):
        return lax.ppermute(v, "feat", [(i, move(i)) for i in range(8)])

    def layer_step(v, move):
        return lax.ppermute(v, "layer", [(i, move(i)) for i in range(32)])

    def swap_cores(v):
        return feat_step(v, lambda i: i ^ 1)

    def along_x(v, d):
        return feat_step(v, lambda i: (i + 2 * d) % 8)

    offset = chosen - feat * feats
    onehot = (offset[:, None] == jnp.arange(feats)[None, :]).astype(BF)

    def picked(side):
        part = lax.dynamic_slice_in_dim(dec, side * half, half, 1)
        return jnp.dot(onehot, part, preferred_element_type=F32).astype(BF)

    away = swap_cores(picked(1 - c))
    mine = picked(c) + away

    def chunk(d):
        return lax.dynamic_slice_in_dim(mine, rows * ((x + d) % 4), rows, 0)

    got = [along_x(chunk(d), d) for d in (1, 2, 3)]
    total = chunk(0).astype(F32)
    for g in got:
        total = total + g.astype(F32)

    before = jnp.zeros_like(total)
    for bit, move in ((1, lambda i: i ^ 1), (2, lambda i: i ^ 2), (4, lambda i: i ^ 7)):
        other = layer_step(total.astype(BF), move).astype(F32)
        before = before + jnp.where((z & bit) != 0, other, 0.0)
        total = total + other
    low = total.astype(BF)
    for d in (1, 2, 3):
        pairs = [(i, i + 8 * d) for i in range(32 - 8 * d)]
        before = before + lax.ppermute(low, "layer", pairs).astype(F32)
    prefix = before.astype(BF)

    whole = jnp.zeros((k, half), BF)
    for d in (0, 1, 2, 3):
        piece = along_x(prefix, d) if d else prefix
        whole = lax.dynamic_update_slice_in_dim(whole, piece, rows * ((x - d) % 4), 0)
    other_half = swap_cores(whole)

    def product(v, side):
        part = lax.dynamic_slice_in_dim(enc, side * half, half, 0)
        return jnp.dot(v, part, preferred_element_type=F32)

    result = product(whole, c) + product(other_half, 1 - c)
    return result.astype(BF)[None]


def solution(mesh):
    placed = (P("layer", None, "feat"), P("layer", "feat", None), P())
    return jax.shard_map(
        local, mesh=mesh, in_specs=placed, out_specs=P("layer", None, "feat"), check_vma=False
    )
```

```python
import jax
import jax.numpy as jnp
from jax import lax
from jax.experimental import pallas as pl
from jax.experimental.pallas import tpu as pltpu
from jax.sharding import PartitionSpec as P

BF = jnp.bfloat16
F32 = jnp.float32
MIB = 2**20
PARTS = 3


def pick_kernel(flip, chosen_ref, dec_ref, out_ref, hot_ref, buf_ref, list_ref, sems):
    k, feats = hot_ref.shape
    half = out_ref.shape[1]
    wide = half // PARTS
    feat = lax.axis_index("feat")
    side = (feat + flip) % 2
    listed = pltpu.make_async_copy(chosen_ref, list_ref, sems.at[PARTS])
    listed.start()
    copies = []
    for p in range(PARTS):
        at = pl.multiple_of(side * half + p * wide, 128)
        copies.append(
            pltpu.make_async_copy(
                dec_ref.at[:, pl.ds(at, wide)], buf_ref.at[:, pl.ds(p * wide, wide)], sems.at[p]
            )
        )
    for copy in copies:
        copy.start()
    listed.wait()
    offset = list_ref[...] - feat * feats
    down = jnp.broadcast_to(offset, (k, k)).T
    lane = lax.broadcasted_iota(jnp.int32, (k, k), 1)
    for j in range(feats // k):
        hot_ref[:, j * k : (j + 1) * k] = (down == lane + j * k).astype(F32).astype(BF)
    for p in range(PARTS):
        cols = slice(p * wide, (p + 1) * wide)
        copies[p].wait()
        out_ref[:, cols] = jnp.dot(hot_ref[...], buf_ref[:, cols], preferred_element_type=F32).astype(BF)


def pick(chosen, dec, flip):
    feats, width = dec.shape
    k, half = chosen.shape[1], width // 2
    return pl.pallas_call(
        lambda *refs: pick_kernel(flip, *refs),
        in_specs=[pl.BlockSpec(memory_space=pltpu.HBM)] * 2,
        out_specs=pl.BlockSpec(memory_space=pltpu.VMEM),
        out_shape=jax.ShapeDtypeStruct((k, half), BF),
        scratch_shapes=[
            pltpu.VMEM((k, feats), BF),
            pltpu.VMEM((feats, half), BF),
            pltpu.VMEM((1, k), jnp.int32),
            pltpu.SemaphoreType.DMA((PARTS + 1,)),
        ],
        compiler_params=pltpu.CompilerParams(vmem_limit_bytes=8 * MIB),
        cost_estimate=pl.CostEstimate(flops=2 * k * feats * half, bytes_accessed=2 * feats * half, transcendentals=0),
        name=f"pick{flip}",
    )(chosen, dec)


def fetch_kernel(enc_ref, out_ref, sem):
    copy = pltpu.make_async_copy(enc_ref, out_ref, sem)
    copy.start()
    copy.wait()


def fetch(enc):
    return pl.pallas_call(
        fetch_kernel,
        in_specs=[pl.BlockSpec(memory_space=pltpu.HBM)],
        out_specs=pl.BlockSpec(memory_space=pltpu.VMEM),
        out_shape=jax.ShapeDtypeStruct(enc.shape, enc.dtype),
        scratch_shapes=[pltpu.SemaphoreType.DMA],
        compiler_params=pltpu.CompilerParams(vmem_limit_bytes=8 * MIB),
        cost_estimate=pl.CostEstimate(flops=0, bytes_accessed=4 * enc.size, transcendentals=0),
        name="fetch",
    )(enc)


def product_kernel(flip, *refs):
    left_ref, enc_ref = refs[:2]
    out_ref = refs[-1]
    half = left_ref.shape[1]
    side = (lax.axis_index("feat") + flip) % 2
    at = pl.multiple_of(side * half, 128)
    tile = 256
    for j in range(out_ref.shape[1] // tile):
        cols = slice(j * tile, (j + 1) * tile)
        part = jnp.dot(left_ref[...], enc_ref[pl.ds(at, half), cols], preferred_element_type=F32)
        if flip:
            part = part + refs[2][:, cols]
        out_ref[:, cols] = part.astype(out_ref.dtype)


def product(left, enc, flip, *more):
    k, half = left.shape
    n = enc.shape[1]
    return pl.pallas_call(
        lambda *refs: product_kernel(flip, *refs),
        in_specs=[pl.BlockSpec(memory_space=pltpu.VMEM)] * (2 + len(more)),
        out_specs=pl.BlockSpec(memory_space=pltpu.VMEM),
        out_shape=jax.ShapeDtypeStruct((k, n), BF if flip else F32),
        compiler_params=pltpu.CompilerParams(vmem_limit_bytes=16 * MIB),
        cost_estimate=pl.CostEstimate(flops=2 * k * n * half, bytes_accessed=2 * half * n, transcendentals=0),
        name=f"product{flip}",
    )(left, enc, *more)


def local(encoder, decoder, chosen):
    enc = pltpu.with_memory_space_constraint(encoder[0], pltpu.HBM)
    dec = pltpu.with_memory_space_constraint(decoder[0], pltpu.HBM)
    k = chosen.shape[0]
    chosen = pltpu.with_memory_space_constraint(chosen.reshape(1, k), pltpu.HBM)
    rows = k // 4
    feat, layer = lax.axis_index("feat"), lax.axis_index("layer")
    x = feat // 2
    y, z = layer // 8, layer % 8

    def feat_step(v, move):
        return lax.ppermute(v, "feat", [(i, move(i)) for i in range(8)])

    def along_x(v, d):
        return feat_step(v, lambda i: (i + 2 * d) % 8)

    def along_z(v, move):
        return lax.ppermute(v, "layer", [(i, i // 8 * 8 + move(i % 8) % 8) for i in range(32)])

    def along_y(v, d):
        return lax.ppermute(v, "layer", [(i, (i + 8 * d) % 32) for i in range(32)])

    away = feat_step(pick(chosen, dec, 1), lambda i: i ^ 1)
    mine = pick(chosen, dec, 0) + away

    def chunk(d):
        return lax.dynamic_slice_in_dim(mine, rows * ((x + d) % 4), rows, 0)

    got = [along_x(chunk(d), d) for d in (2, 1, 3)]
    total = chunk(0).astype(F32)
    for g in got:
        total = total + g.astype(F32)

    near = fetch(enc)

    before = jnp.zeros_like(total)

    def join(arrivals, before, total):
        for lower, v in arrivals:
            v = v.astype(F32)
            before = before + jnp.where(lower, v, 0.0)
            total = total + v
        return before, total

    before, total = join([(z % 2 == 1, along_z(total.astype(BF), lambda i: i ^ 1))], before, total)
    low = total.astype(BF)
    across = along_z(low, lambda i: i + 3 if i % 2 else i - 3)
    up = along_z(low, lambda i: i + 2)
    down = along_z(low, lambda i: i - 2)
    before, total = join([(z >= 4, across), (z >= 2, up), (z >= 6, down)], before, total)
    low = total.astype(BF)
    arrivals = [(y >= d, along_y(low, d)) for d in (2, 1, 3)]
    before, total = join(arrivals, before, total)
    prefix, near = lax.optimization_barrier((before.astype(BF), near))

    whole = jnp.zeros((k, prefix.shape[1]), BF)
    for d in (0, 2, 1, 3):
        piece = along_x(prefix, d) if d else prefix
        whole = lax.dynamic_update_slice_in_dim(whole, piece, rows * ((x + 4 - d) % 4), 0)
    other = feat_step(whole, lambda i: i ^ 1)
    result = product(other, near, 1, product(whole, near, 0))
    return result[None]


def solution(mesh):
    placed = (P("layer", None, "feat"), P("layer", "feat", None), P())
    return jax.shard_map(
        local, mesh=mesh, in_specs=placed, out_specs=P("layer", None, "feat"), check_vma=False
    )
```

```python
import jax
import jax.numpy as jnp
from jax import lax
from jax.experimental import pallas as pl
from jax.experimental.pallas import tpu as pltpu
from jax.sharding import PartitionSpec as P

BF = jnp.bfloat16
F32 = jnp.float32
MIB = 2**20
PARTS = 3


def pick_kernel(flip, chosen_ref, dec_ref, out_ref, hot_ref, buf_ref, list_ref, sems):
    k, feats = hot_ref.shape
    half = out_ref.shape[1]
    wide = half // PARTS
    feat = lax.axis_index("feat")
    side = (feat + flip) % 2
    listed = pltpu.make_async_copy(chosen_ref, list_ref, sems.at[PARTS])
    listed.start()
    copies = []
    for p in range(PARTS):
        at = pl.multiple_of(side * half + p * wide, 128)
        copies.append(
            pltpu.make_async_copy(
                dec_ref.at[:, pl.ds(at, wide)], buf_ref.at[:, pl.ds(p * wide, wide)], sems.at[p]
            )
        )
    for copy in copies:
        copy.start()
    listed.wait()
    offset = list_ref[...] - feat * feats
    down = jnp.broadcast_to(offset, (k, k)).T
    lane = lax.broadcasted_iota(jnp.int32, (k, k), 1)
    for j in range(feats // k):
        hot_ref[:, j * k : (j + 1) * k] = (down == lane + j * k).astype(F32).astype(BF)
    for p in range(PARTS):
        cols = slice(p * wide, (p + 1) * wide)
        copies[p].wait()
        out_ref[:, cols] = jnp.dot(hot_ref[...], buf_ref[:, cols], preferred_element_type=F32).astype(BF)


def pick(chosen, dec, flip):
    feats, width = dec.shape
    k, half = chosen.shape[1], width // 2
    return pl.pallas_call(
        lambda *refs: pick_kernel(flip, *refs),
        in_specs=[pl.BlockSpec(memory_space=pltpu.HBM)] * 2,
        out_specs=pl.BlockSpec(memory_space=pltpu.VMEM),
        out_shape=jax.ShapeDtypeStruct((k, half), BF),
        scratch_shapes=[
            pltpu.VMEM((k, feats), BF),
            pltpu.VMEM((feats, half), BF),
            pltpu.VMEM((1, k), jnp.int32),
            pltpu.SemaphoreType.DMA((PARTS + 1,)),
        ],
        compiler_params=pltpu.CompilerParams(vmem_limit_bytes=8 * MIB),
        cost_estimate=pl.CostEstimate(flops=2 * k * feats * half, bytes_accessed=2 * feats * half, transcendentals=0),
        name=f"pick{flip}",
    )(chosen, dec)


def fetch_kernel(own_ref, enc_ref, out_ref, same_ref, sem):
    copy = pltpu.make_async_copy(enc_ref, out_ref, sem)
    copy.start()
    same_ref[...] = own_ref[...]
    copy.wait()


def fetch(own, enc):
    return pl.pallas_call(
        fetch_kernel,
        in_specs=[pl.BlockSpec(memory_space=pltpu.VMEM), pl.BlockSpec(memory_space=pltpu.HBM)],
        out_specs=[pl.BlockSpec(memory_space=pltpu.VMEM)] * 2,
        out_shape=[pltpu.VMEM(enc.shape, enc.dtype), jax.ShapeDtypeStruct(own.shape, own.dtype)],
        scratch_shapes=[pltpu.SemaphoreType.DMA],
        compiler_params=pltpu.CompilerParams(vmem_limit_bytes=8 * MIB),
        cost_estimate=pl.CostEstimate(flops=0, bytes_accessed=4 * enc.size, transcendentals=0),
        name="fetch",
    )(own, enc)


def product_kernel(flip, *refs):
    left_ref, enc_ref = refs[:2]
    out_ref = refs[-1]
    half = left_ref.shape[1]
    side = (lax.axis_index("feat") + flip) % 2
    at = pl.multiple_of(side * half, 128)
    tile = 256
    for j in range(out_ref.shape[1] // tile):
        cols = slice(j * tile, (j + 1) * tile)
        part = jnp.dot(left_ref[...], enc_ref[pl.ds(at, half), cols], preferred_element_type=F32)
        if flip:
            part = part + refs[2][:, cols]
        out_ref[:, cols] = part.astype(out_ref.dtype)


def product(left, enc, flip, *more):
    k, half = left.shape
    n = enc.shape[1]
    return pl.pallas_call(
        lambda *refs: product_kernel(flip, *refs),
        in_specs=[pl.BlockSpec(memory_space=pltpu.VMEM)] * (2 + len(more)),
        out_specs=pl.BlockSpec(memory_space=pltpu.VMEM),
        out_shape=jax.ShapeDtypeStruct((k, n), BF if flip else F32),
        compiler_params=pltpu.CompilerParams(vmem_limit_bytes=16 * MIB),
        cost_estimate=pl.CostEstimate(flops=2 * k * n * half, bytes_accessed=2 * half * n, transcendentals=0),
        name=f"product{flip}",
    )(left, enc, *more)


def local(encoder, decoder, chosen):
    enc = pltpu.with_memory_space_constraint(encoder[0], pltpu.HBM)
    dec = pltpu.with_memory_space_constraint(decoder[0], pltpu.HBM)
    k = chosen.shape[0]
    chosen = pltpu.with_memory_space_constraint(chosen.reshape(1, k), pltpu.HBM)
    rows = k // 4
    feat, layer = lax.axis_index("feat"), lax.axis_index("layer")
    x = feat // 2
    y, z = layer // 8, layer % 8

    def feat_step(v, move):
        return lax.ppermute(v, "feat", [(i, move(i)) for i in range(8)])

    def along_x(v, d):
        return feat_step(v, lambda i: (i + 2 * d) % 8)

    def along_z(v, move):
        return lax.ppermute(v, "layer", [(i, i // 8 * 8 + move(i % 8) % 8) for i in range(32)])

    def along_y(v, d):
        return lax.ppermute(v, "layer", [(i, (i + 8 * d) % 32) for i in range(32)])

    away = feat_step(pick(chosen, dec, 1), lambda i: i ^ 1)
    mine = pick(chosen, dec, 0) + away

    def chunk(d):
        return lax.dynamic_slice_in_dim(mine, rows * ((x + d) % 4), rows, 0)

    got = [along_x(chunk(d), d) for d in (1, 3, 2)]
    total = chunk(0).astype(F32)
    for g in got:
        total = total + g.astype(F32)

    before = jnp.zeros_like(total)

    def join(arrivals, before, total):
        for lower, v in arrivals:
            v = v.astype(F32)
            before = before + jnp.where(lower, v, 0.0)
            total = total + v
        return before, total

    before, total = join([(z % 2 == 1, along_z(total.astype(BF), lambda i: i ^ 1))], before, total)
    low = total.astype(BF)
    up = along_z(low, lambda i: i + 2)
    down = along_z(low, lambda i: i - 2)
    across = along_z(low, lambda i: i + 3 if i % 2 else i - 3)
    before, total = join([(z >= 4, across), (z >= 2, up), (z >= 6, down)], before, total)
    low = total.astype(BF)
    arrivals = [(y >= d, along_y(low, d)) for d in (1, 3, 2)]
    before, total = join(arrivals, before, total)
    prefix = before.astype(BF)

    pieces = [along_x(prefix, d) for d in (1, 3, 2)]
    near, prefix = fetch(prefix, enc)
    whole = jnp.zeros((k, prefix.shape[1]), BF)
    for d, piece in zip((0, 1, 3, 2), [prefix] + pieces):
        whole = lax.dynamic_update_slice_in_dim(whole, piece, rows * ((x + 4 - d) % 4), 0)
    other = feat_step(whole, lambda i: i ^ 1)
    result = product(other, near, 1, product(whole, near, 0))
    return result[None]


def solution(mesh):
    placed = (P("layer", None, "feat"), P("layer", "feat", None), P())
    return jax.shard_map(
        local, mesh=mesh, in_specs=placed, out_specs=P("layer", None, "feat"), check_vma=False
    )
```

```python
import jax
import jax.numpy as jnp
from jax import lax
from jax.experimental import pallas as pl
from jax.experimental.pallas import tpu as pltpu
from jax.sharding import PartitionSpec as P

BF = jnp.bfloat16
F32 = jnp.float32
I32 = jnp.int32
MIB = 2**20
PARTS = 6
FEATS = 8
LAYERS = 32


def iota(shape, axis):
    return lax.broadcasted_iota(I32, shape, axis)


def ranks_of(chosen):
    k = chosen.shape[1]
    along = jnp.broadcast_to(chosen, (k, k))
    down = along.T
    row, lane = iota((k, k), 0), iota((k, k), 1)
    b_first = (along < down) | ((along == down) & (lane < row))
    a_first = (down < along) | ((along == down) & (row < lane))
    rank_down = jnp.sum(b_first.astype(F32), axis=1, keepdims=True)
    rank_along = jnp.sum(a_first.astype(F32), axis=0, keepdims=True)
    return rank_down, rank_along


def slots_onehot(chosen, rank_along, first, n, base, hot_ref):
    k = chosen.shape[1]
    feats = hot_ref.shape[1]
    slot = (first + iota((n, k), 0)).astype(F32)
    here = jnp.broadcast_to(rank_along, (n, k)) == slot
    value = jnp.where(here, jnp.broadcast_to(chosen.astype(F32) + 1.0, (n, k)), 0.0)
    feature = jnp.sum(value, axis=1, keepdims=True) - 1.0 - base.astype(F32)
    feature = jnp.broadcast_to(feature, (n, k))
    lane = iota((n, k), 1).astype(F32)
    for j in range(feats // k):
        hot_ref[:, j * k : (j + 1) * k] = (feature == lane + float(j * k)).astype(F32).astype(BF)


def pick_kernel(near, chosen_ref, dec_ref, *refs):
    outs, (hot_ref, buf_ref, list_ref, sems) = refs[:-4], refs[-4:]
    n, feats = hot_ref.shape
    k = list_ref.shape[1]
    width = buf_ref.shape[1]
    wide = width // PARTS
    share = k // FEATS
    feat = lax.axis_index("feat")
    listed = pltpu.make_async_copy(chosen_ref, list_ref, sems.at[PARTS])
    listed.start()
    copies = []
    for p in range(PARTS):
        cols = pl.ds(p * wide, wide)
        copies.append(pltpu.make_async_copy(dec_ref.at[:, cols], buf_ref.at[:, cols], sems.at[p]))
        copies[p].start()
    listed.wait()
    chosen = list_ref[...]
    rank_down, rank_along = ranks_of(chosen)
    first = share * (feat - 1) if near else 0
    slots_onehot(chosen, rank_along, first, n, feat * feats, hot_ref)
    if near:
        p = iota((k, k), 1)
        half = k // 2
        other, rest = lax.div(p, half), lax.rem(p, half)
        owner = 2 * lax.div(rest, share) + lax.rem(feat + other, 2)
        slot = share * owner + lax.rem(rest, share)
        order = jnp.broadcast_to(rank_down, (k, k)) == slot.astype(F32)
        outs[3][...] = order.astype(F32).astype(BF)
        edge = iota((FEATS, k), 0)
        held = jnp.sum((jnp.broadcast_to(chosen, (FEATS, k)) < edge * feats).astype(F32), axis=1, keepdims=True)
        far = jnp.abs(held - (edge[:, :1] * share).astype(F32)) > share
        outs[4][...] = jnp.broadcast_to(jnp.max(far.astype(F32), axis=0, keepdims=True), outs[4].shape)
    for p in range(PARTS):
        cols = slice(p * wide, (p + 1) * wide)
        copies[p].wait()
        part = jnp.dot(hot_ref[...], buf_ref[:, cols], preferred_element_type=F32).astype(BF)
        if near:
            for i in range(3):
                outs[i][:, cols] = part[i * share : (i + 1) * share]
        else:
            outs[0][:, cols] = part


def pick(chosen, dec, near):
    feats, width = dec.shape
    k = chosen.shape[1]
    share = k // FEATS
    n = 3 * share if near else k
    if near:
        shapes = [(share, width)] * 3 + [(k, k), (8, 128), (share, width)]
        shapes = [jax.ShapeDtypeStruct(shape, F32 if shape[0] == 8 else BF) for shape in shapes]
        spaces = [pltpu.VMEM] * 5 + [pltpu.HBM]
    else:
        shapes, spaces = [jax.ShapeDtypeStruct((k, width), BF)], [pltpu.VMEM]
    return pl.pallas_call(
        lambda *refs: pick_kernel(near, *refs),
        in_specs=[pl.BlockSpec(memory_space=pltpu.HBM)] * 2,
        out_specs=[pl.BlockSpec(memory_space=space) for space in spaces],
        out_shape=shapes,
        scratch_shapes=[
            pltpu.VMEM((n, feats), BF),
            pltpu.VMEM((feats, width), BF),
            pltpu.VMEM((1, k), I32),
            pltpu.SemaphoreType.DMA((PARTS + 1,)),
        ],
        compiler_params=pltpu.CompilerParams(vmem_limit_bytes=12 * MIB),
        cost_estimate=pl.CostEstimate(flops=2 * n * feats * width, bytes_accessed=2 * feats * width, transcendentals=0),
        name="pick_near" if near else "pick_all",
    )(chosen, dec)


def settle_kernel(own_ref, up_ref, down_ref, far_ref, room_ref, out_ref, sem):
    far = far_ref[0, 0] > 0.0

    @pl.when(far)
    def _():
        copy = pltpu.make_async_copy(room_ref, out_ref, sem)
        copy.start()
        copy.wait()

    @pl.when(jnp.logical_not(far))
    def _():
        out_ref[...] = own_ref[...] + up_ref[...] + down_ref[...]


def settle(own, up, down, far, room):
    return pl.pallas_call(
        settle_kernel,
        in_specs=[pl.BlockSpec(memory_space=pltpu.VMEM)] * 4 + [pl.BlockSpec(memory_space=pltpu.HBM)],
        out_specs=pl.BlockSpec(memory_space=pltpu.VMEM),
        out_shape=jax.ShapeDtypeStruct(own.shape, own.dtype),
        scratch_shapes=[pltpu.SemaphoreType.DMA],
        compiler_params=pltpu.CompilerParams(vmem_limit_bytes=2 * MIB),
        cost_estimate=pl.CostEstimate(flops=2 * own.size, bytes_accessed=8 * own.size, transcendentals=0),
        name="settle",
    )(own, up, down, far, room)


def fetch_kernel(own_ref, enc_ref, out_ref, same_ref, sem):
    copy = pltpu.make_async_copy(enc_ref, out_ref, sem)
    copy.start()
    same_ref[...] = own_ref[...]
    copy.wait()


def fetch(own, enc):
    return pl.pallas_call(
        fetch_kernel,
        in_specs=[pl.BlockSpec(memory_space=pltpu.VMEM), pl.BlockSpec(memory_space=pltpu.HBM)],
        out_specs=[pl.BlockSpec(memory_space=pltpu.VMEM)] * 2,
        out_shape=[pltpu.VMEM(enc.shape, enc.dtype), jax.ShapeDtypeStruct(own.shape, own.dtype)],
        scratch_shapes=[pltpu.SemaphoreType.DMA],
        compiler_params=pltpu.CompilerParams(vmem_limit_bytes=8 * MIB),
        cost_estimate=pl.CostEstimate(flops=0, bytes_accessed=4 * enc.size, transcendentals=0),
        name="fetch",
    )(own, enc)


def product_kernel(last, left_ref, enc_ref, *refs):
    half = left_ref.shape[0]
    if last:
        first_ref, order_ref, out_ref, rows_ref = refs
        rows_ref[:half, :] = first_ref[...]
    else:
        out_ref = rows_ref = refs[0]
    at = half if last else 0
    tile = 256
    for j in range(out_ref.shape[1] // tile):
        cols = slice(j * tile, (j + 1) * tile)
        part = jnp.dot(left_ref[...], enc_ref[:, cols], preferred_element_type=F32)
        rows_ref[at : at + half, cols] = part.astype(BF)
    if last:
        for j in range(out_ref.shape[1] // tile):
            cols = slice(j * tile, (j + 1) * tile)
            part = jnp.dot(order_ref[...], rows_ref[:, cols], preferred_element_type=F32)
            out_ref[:, cols] = part.astype(BF)


def product(left, enc, *more):
    half, width = left.shape
    n = enc.shape[1]
    last = bool(more)
    return pl.pallas_call(
        lambda *refs: product_kernel(last, *refs),
        in_specs=[pl.BlockSpec(memory_space=pltpu.VMEM)] * (2 + len(more)),
        out_specs=pl.BlockSpec(memory_space=pltpu.VMEM),
        out_shape=jax.ShapeDtypeStruct((2 * half if last else half, n), BF),
        scratch_shapes=[pltpu.VMEM((2 * half, n), BF)] if last else [],
        compiler_params=pltpu.CompilerParams(vmem_limit_bytes=16 * MIB),
        cost_estimate=pl.CostEstimate(flops=2 * half * n * width, bytes_accessed=2 * width * n, transcendentals=0),
        name="product_last" if last else "product_own",
    )(left, enc, *more)


def local(encoder, decoder, chosen):
    enc = pltpu.with_memory_space_constraint(encoder[0], pltpu.HBM)
    dec = pltpu.with_memory_space_constraint(decoder[0], pltpu.HBM)
    k, feats = chosen.shape[0], dec.shape[0]
    share = k // FEATS
    listed = pltpu.with_memory_space_constraint(chosen.reshape(1, k), pltpu.HBM)
    feat, layer = lax.axis_index("feat"), lax.axis_index("layer")
    x = feat // 2
    y, z = layer // 8, layer % 8

    def feat_step(v, move):
        return lax.ppermute(v, "feat", [(i, move(i) % FEATS) for i in range(FEATS)])

    def along_x(v, d):
        return feat_step(v, lambda i: i + 2 * d)

    def along_z(v, move):
        return lax.ppermute(v, "layer", [(i, i // 8 * 8 + move(i % 8) % 8) for i in range(LAYERS)])

    def along_y(v, d):
        return lax.ppermute(v, "layer", [(i, (i + 8 * d) % LAYERS) for i in range(LAYERS)])

    below, own, above, order, far, room = pick(listed, dec, True)
    up = feat_step(above, lambda i: i + 1)
    down = feat_step(below, lambda i: i - 1)

    def general(state):
        (rows,) = pick(listed, dec, False)

        def chunk(d):
            return lax.dynamic_slice_in_dim(rows, share * ((feat + d) % FEATS), share, 0)

        total = chunk(0)
        for d in range(1, FEATS):
            total = total + feat_step(chunk(d), lambda i: i + d)
        return jnp.zeros_like(state[0]), total

    edges = jnp.arange(1, FEATS)
    held = jnp.sum((chosen[:, None] < edges[None, :] * feats).astype(I32), axis=0)
    spread = jnp.any(jnp.abs(held - edges * share) > share)
    room = lax.while_loop(lambda state: state[0], general, (spread, room))[1]
    total = settle(own, up, down, far, room).astype(F32)

    before = jnp.zeros_like(total)

    def join(arrivals, before, total):
        for lower, v in arrivals:
            v = v.astype(F32)
            before = before + jnp.where(lower, v, 0.0)
            total = total + v
        return before, total

    before, total = join([(z % 2 == 1, along_z(total.astype(BF), lambda i: i ^ 1))], before, total)
    low = total.astype(BF)
    up = along_z(low, lambda i: i + 2)
    down = along_z(low, lambda i: i - 2)
    across = along_z(low, lambda i: i + 3 if i % 2 else i - 3)
    before, total = join([(z >= 4, across), (z >= 2, up), (z >= 6, down)], before, total)
    low = total.astype(BF)
    arrivals = [(y >= d, along_y(low, d)) for d in (1, 3, 2)]
    before, total = join(arrivals, before, total)
    prefix = before.astype(BF)

    pieces = [along_x(prefix, d) for d in (1, 3, 2)]
    near, prefix = fetch(prefix, enc)
    whole = jnp.zeros((k // 2, prefix.shape[1]), BF)
    for d, piece in zip((0, 1, 3, 2), [prefix] + pieces):
        whole = lax.dynamic_update_slice_in_dim(whole, piece, share * ((x + 4 - d) % 4), 0)
    other = feat_step(whole, lambda i: i ^ 1)
    return product(other, near, product(whole, near), order)[None]


def solution(mesh):
    placed = (P("layer", None, "feat"), P("layer", "feat", None), P())
    return jax.shard_map(
        local, mesh=mesh, in_specs=placed, out_specs=P("layer", None, "feat"), check_vma=False
    )
```

```python
import jax
import jax.numpy as jnp
from jax import lax
from jax.experimental import pallas as pl
from jax.experimental.pallas import tpu as pltpu
from jax.sharding import PartitionSpec as P

BF = jnp.bfloat16
F32 = jnp.float32
I32 = jnp.int32
MIB = 2**20
PARTS = 6
FEATS = 8
LAYERS = 32


def iota(shape, axis):
    return lax.broadcasted_iota(I32, shape, axis)


def ranks_of(chosen):
    k = chosen.shape[1]
    along = jnp.broadcast_to(chosen, (k, k))
    down = along.T
    row, lane = iota((k, k), 0), iota((k, k), 1)
    b_first = (along < down) | ((along == down) & (lane < row))
    a_first = (down < along) | ((along == down) & (row < lane))
    rank_down = jnp.sum(b_first.astype(F32), axis=1, keepdims=True)
    rank_along = jnp.sum(a_first.astype(F32), axis=0, keepdims=True)
    return rank_down, rank_along


def slots_onehot(chosen, rank_along, first, n, base, hot_ref):
    k = chosen.shape[1]
    feats = hot_ref.shape[1]
    slot = (first + iota((n, k), 0)).astype(F32)
    here = jnp.broadcast_to(rank_along, (n, k)) == slot
    value = jnp.where(here, jnp.broadcast_to(chosen.astype(F32) + 1.0, (n, k)), 0.0)
    feature = jnp.sum(value, axis=1, keepdims=True) - 1.0 - base.astype(F32)
    feature = jnp.broadcast_to(feature, (n, k))
    lane = iota((n, k), 1).astype(F32)
    for j in range(feats // k):
        hot_ref[:, j * k : (j + 1) * k] = (feature == lane + float(j * k)).astype(F32).astype(BF)


def pick_kernel(near, chosen_ref, dec_ref, *refs):
    outs, (hot_ref, buf_ref, list_ref, sems) = refs[:-4], refs[-4:]
    n, feats = hot_ref.shape
    k = list_ref.shape[1]
    width = buf_ref.shape[1]
    wide = width // PARTS
    share = k // FEATS
    feat = lax.axis_index("feat")
    listed = pltpu.make_async_copy(chosen_ref, list_ref, sems.at[PARTS])
    listed.start()
    copies = []
    for p in range(PARTS):
        cols = pl.ds(p * wide, wide)
        copies.append(pltpu.make_async_copy(dec_ref.at[:, cols], buf_ref.at[:, cols], sems.at[p]))
        copies[p].start()
    listed.wait()
    chosen = list_ref[...]
    rank_down, rank_along = ranks_of(chosen)
    first = share * (feat - 1) if near else 0
    slots_onehot(chosen, rank_along, first, n, feat * feats, hot_ref)
    if near:
        p = iota((k, k), 1)
        half = k // 2
        other, rest = lax.div(p, half), lax.rem(p, half)
        owner = 2 * lax.div(rest, share) + lax.rem(feat + other, 2)
        slot = share * owner + lax.rem(rest, share)
        order = jnp.broadcast_to(rank_down, (k, k)) == slot.astype(F32)
        outs[3][...] = order.astype(F32).astype(BF)
        edge = iota((FEATS, k), 0)
        held = jnp.sum((jnp.broadcast_to(chosen, (FEATS, k)) < edge * feats).astype(F32), axis=1, keepdims=True)
        far = jnp.abs(held - (edge[:, :1] * share).astype(F32)) > share
        outs[4][...] = jnp.broadcast_to(jnp.max(far.astype(F32), axis=0, keepdims=True), outs[4].shape)
    for p in range(PARTS):
        cols = slice(p * wide, (p + 1) * wide)
        copies[p].wait()
        part = jnp.dot(hot_ref[...], buf_ref[:, cols], preferred_element_type=F32).astype(BF)
        if near:
            for i in range(3):
                outs[i][:, cols] = part[i * share : (i + 1) * share]
        else:
            outs[0][:, cols] = part


def pick(chosen, dec, near):
    feats, width = dec.shape
    k = chosen.shape[1]
    share = k // FEATS
    n = 3 * share if near else k
    if near:
        shapes = [(share, width)] * 3 + [(k, k), (8, 128), (share, width)]
        shapes = [jax.ShapeDtypeStruct(shape, F32 if shape[0] == 8 else BF) for shape in shapes]
        shapes[-1] = pltpu.HBM((share, width), BF)
        spaces = [pltpu.VMEM] * 5 + [pltpu.HBM]
    else:
        shapes, spaces = [jax.ShapeDtypeStruct((k, width), BF)], [pltpu.VMEM]
    return pl.pallas_call(
        lambda *refs: pick_kernel(near, *refs),
        in_specs=[pl.BlockSpec(memory_space=pltpu.HBM)] * 2,
        out_specs=[pl.BlockSpec(memory_space=space) for space in spaces],
        out_shape=shapes,
        scratch_shapes=[
            pltpu.VMEM((n, feats), BF),
            pltpu.VMEM((feats, width), BF),
            pltpu.VMEM((1, k), I32),
            pltpu.SemaphoreType.DMA((PARTS + 1,)),
        ],
        compiler_params=pltpu.CompilerParams(vmem_limit_bytes=12 * MIB),
        cost_estimate=pl.CostEstimate(flops=2 * n * feats * width, bytes_accessed=2 * feats * width, transcendentals=0),
        name="pick_near" if near else "pick_all",
    )(chosen, dec)


def after(up, down, room):
    return pl.pallas_call(
        lambda up_ref, down_ref, room_ref, out_ref: None,
        in_specs=[pl.BlockSpec(memory_space=pltpu.VMEM)] * 2 + [pl.BlockSpec(memory_space=pltpu.HBM)],
        out_specs=pl.BlockSpec(memory_space=pltpu.HBM),
        out_shape=pltpu.HBM(room.shape, room.dtype),
        input_output_aliases={2: 0},
        compiler_params=pltpu.CompilerParams(vmem_limit_bytes=MIB),
        name="after",
    )(up, down, pltpu.with_memory_space_constraint(room, pltpu.HBM))


def settle_kernel(own_ref, up_ref, down_ref, far_ref, room_ref, out_ref, sem):
    far = far_ref[0, 0] > 0.0

    @pl.when(far)
    def _():
        copy = pltpu.make_async_copy(room_ref, out_ref, sem)
        copy.start()
        copy.wait()

    @pl.when(jnp.logical_not(far))
    def _():
        out_ref[...] = own_ref[...] + up_ref[...] + down_ref[...]


def settle(own, up, down, far, room):
    return pl.pallas_call(
        settle_kernel,
        in_specs=[pl.BlockSpec(memory_space=pltpu.VMEM)] * 4 + [pl.BlockSpec(memory_space=pltpu.HBM)],
        out_specs=pl.BlockSpec(memory_space=pltpu.VMEM),
        out_shape=jax.ShapeDtypeStruct(own.shape, own.dtype),
        scratch_shapes=[pltpu.SemaphoreType.DMA],
        compiler_params=pltpu.CompilerParams(vmem_limit_bytes=2 * MIB),
        cost_estimate=pl.CostEstimate(flops=2 * own.size, bytes_accessed=8 * own.size, transcendentals=0),
        name="settle",
    )(own, up, down, far, room)


def fetch_kernel(own_ref, enc_ref, out_ref, same_ref, sem):
    copy = pltpu.make_async_copy(enc_ref, out_ref, sem)
    copy.start()
    same_ref[...] = own_ref[...]
    copy.wait()


def fetch(own, enc):
    return pl.pallas_call(
        fetch_kernel,
        in_specs=[pl.BlockSpec(memory_space=pltpu.VMEM), pl.BlockSpec(memory_space=pltpu.HBM)],
        out_specs=[pl.BlockSpec(memory_space=pltpu.VMEM)] * 2,
        out_shape=[pltpu.VMEM(enc.shape, enc.dtype), jax.ShapeDtypeStruct(own.shape, own.dtype)],
        scratch_shapes=[pltpu.SemaphoreType.DMA],
        compiler_params=pltpu.CompilerParams(vmem_limit_bytes=8 * MIB),
        cost_estimate=pl.CostEstimate(flops=0, bytes_accessed=4 * enc.size, transcendentals=0),
        name="fetch",
    )(own, enc)


def product_kernel(last, left_ref, enc_ref, *refs):
    half = left_ref.shape[0]
    if last:
        first_ref, order_ref, out_ref, rows_ref = refs
        rows_ref[:half, :] = first_ref[...]
    else:
        out_ref = rows_ref = refs[0]
    at = half if last else 0
    tile = 256
    for j in range(out_ref.shape[1] // tile):
        cols = slice(j * tile, (j + 1) * tile)
        part = jnp.dot(left_ref[...], enc_ref[:, cols], preferred_element_type=F32)
        rows_ref[at : at + half, cols] = part.astype(BF)
    if last:
        for j in range(out_ref.shape[1] // tile):
            cols = slice(j * tile, (j + 1) * tile)
            part = jnp.dot(order_ref[...], rows_ref[:, cols], preferred_element_type=F32)
            out_ref[:, cols] = part.astype(BF)


def product(left, enc, *more):
    half, width = left.shape
    n = enc.shape[1]
    last = bool(more)
    return pl.pallas_call(
        lambda *refs: product_kernel(last, *refs),
        in_specs=[pl.BlockSpec(memory_space=pltpu.VMEM)] * (2 + len(more)),
        out_specs=pl.BlockSpec(memory_space=pltpu.VMEM),
        out_shape=jax.ShapeDtypeStruct((2 * half if last else half, n), BF),
        scratch_shapes=[pltpu.VMEM((2 * half, n), BF)] if last else [],
        compiler_params=pltpu.CompilerParams(vmem_limit_bytes=16 * MIB),
        cost_estimate=pl.CostEstimate(flops=2 * half * n * width, bytes_accessed=2 * width * n, transcendentals=0),
        name="product_last" if last else "product_own",
    )(left, enc, *more)


def local(encoder, decoder, chosen):
    enc = pltpu.with_memory_space_constraint(encoder[0], pltpu.HBM)
    dec = pltpu.with_memory_space_constraint(decoder[0], pltpu.HBM)
    k, feats = chosen.shape[0], dec.shape[0]
    share = k // FEATS
    listed = pltpu.with_memory_space_constraint(chosen.reshape(1, k), pltpu.HBM)
    feat, layer = lax.axis_index("feat"), lax.axis_index("layer")
    x = feat // 2
    y, z = layer // 8, layer % 8

    def feat_step(v, move):
        return lax.ppermute(v, "feat", [(i, move(i) % FEATS) for i in range(FEATS)])

    def along_x(v, d):
        return feat_step(v, lambda i: i + 2 * d)

    def along_z(v, move):
        return lax.ppermute(v, "layer", [(i, i // 8 * 8 + move(i % 8) % 8) for i in range(LAYERS)])

    def along_y(v, d):
        return lax.ppermute(v, "layer", [(i, (i + 8 * d) % LAYERS) for i in range(LAYERS)])

    below, own, above, order, far, room = pick(listed, dec, True)
    up = feat_step(above, lambda i: i + 1)
    down = feat_step(below, lambda i: i - 1)

    def general(state):
        (rows,) = pick(listed, dec, False)

        def chunk(d):
            return lax.dynamic_slice_in_dim(rows, share * ((feat + d) % FEATS), share, 0)

        total = chunk(0)
        for d in range(1, FEATS):
            total = total + feat_step(chunk(d), lambda i: i + d)
        return jnp.zeros_like(state[0]), total

    edges = jnp.arange(1, FEATS)
    held = jnp.sum((chosen[:, None] < edges[None, :] * feats).astype(I32), axis=0)
    close = jnp.all(jnp.abs(held - edges * share) <= share)
    room = lax.while_loop(lambda state: state[0], general, (jnp.logical_not(close), after(up, down, room)))[1]
    total = settle(own, up, down, far, room).astype(F32)

    before = jnp.zeros_like(total)

    def join(arrivals, before, total):
        for lower, v in arrivals:
            v = v.astype(F32)
            before = before + jnp.where(lower, v, 0.0)
            total = total + v
        return before, total

    before, total = join([(z % 2 == 1, along_z(total.astype(BF), lambda i: i ^ 1))], before, total)
    low = total.astype(BF)
    up = along_z(low, lambda i: i + 2)
    down = along_z(low, lambda i: i - 2)
    across = along_z(low, lambda i: i + 3 if i % 2 else i - 3)
    before, total = join([(z >= 4, across), (z >= 2, up), (z >= 6, down)], before, total)
    low = total.astype(BF)
    arrivals = [(y >= d, along_y(low, d)) for d in (1, 3, 2)]
    before, total = join(arrivals, before, total)
    prefix = before.astype(BF)

    pieces = [along_x(prefix, d) for d in (1, 3, 2)]
    near, prefix = fetch(prefix, enc)
    whole = jnp.zeros((k // 2, prefix.shape[1]), BF)
    for d, piece in zip((0, 1, 3, 2), [prefix] + pieces):
        whole = lax.dynamic_update_slice_in_dim(whole, piece, share * ((x + 4 - d) % 4), 0)
    other = feat_step(whole, lambda i: i ^ 1)
    return product(other, near, product(whole, near), order)[None]


def solution(mesh):
    placed = (P("layer", None, "feat"), P("layer", "feat", None), P())
    return jax.shard_map(
        local, mesh=mesh, in_specs=placed, out_specs=P("layer", None, "feat"), check_vma=False
    )
```

```python
import jax
import jax.numpy as jnp
from jax import lax
from jax.experimental import pallas as pl
from jax.experimental.pallas import tpu as pltpu
from jax.sharding import PartitionSpec as P

BF = jnp.bfloat16
F32 = jnp.float32
I32 = jnp.int32
MIB = 2**20
PARTS = 6
FEATS = 8
LAYERS = 32


def iota(shape, axis):
    return lax.broadcasted_iota(I32, shape, axis)


def ranks_of(chosen):
    k = chosen.shape[1]
    along = jnp.broadcast_to(chosen, (k, k))
    down = along.T
    row, lane = iota((k, k), 0), iota((k, k), 1)
    b_first = (along < down) | ((along == down) & (lane < row))
    a_first = (down < along) | ((along == down) & (row < lane))
    rank_down = jnp.sum(b_first.astype(F32), axis=1, keepdims=True)
    rank_along = jnp.sum(a_first.astype(F32), axis=0, keepdims=True)
    return rank_down, rank_along


def slots_onehot(chosen, rank_along, first, n, base, hot_ref):
    k = chosen.shape[1]
    feats = hot_ref.shape[1]
    slot = (first + iota((n, k), 0)).astype(F32)
    here = jnp.broadcast_to(rank_along, (n, k)) == slot
    value = jnp.where(here, jnp.broadcast_to(chosen.astype(F32) + 1.0, (n, k)), 0.0)
    feature = jnp.sum(value, axis=1, keepdims=True) - 1.0 - base.astype(F32)
    feature = jnp.broadcast_to(feature, (n, k))
    lane = iota((n, k), 1).astype(F32)
    for j in range(feats // k):
        hot_ref[:, j * k : (j + 1) * k] = (feature == lane + float(j * k)).astype(F32).astype(BF)


def pick_kernel(near, chosen_ref, dec_ref, *refs):
    outs, (hot_ref, buf_ref, list_ref, sems) = refs[:-4], refs[-4:]
    n, feats = hot_ref.shape
    k = list_ref.shape[1]
    width = buf_ref.shape[1]
    wide = width // PARTS
    share = k // FEATS
    feat = lax.axis_index("feat")
    listed = pltpu.make_async_copy(chosen_ref, list_ref, sems.at[PARTS])
    listed.start()
    copies = []
    for p in range(PARTS):
        cols = pl.ds(p * wide, wide)
        copies.append(pltpu.make_async_copy(dec_ref.at[:, cols], buf_ref.at[:, cols], sems.at[p]))
        copies[p].start()
    listed.wait()
    chosen = list_ref[...]
    rank_down, rank_along = ranks_of(chosen)
    first = share * (feat - 1) if near else 0
    slots_onehot(chosen, rank_along, first, n, feat * feats, hot_ref)
    if near:
        p = iota((k, k), 1)
        half = k // 2
        other, rest = lax.div(p, half), lax.rem(p, half)
        owner = 2 * lax.div(rest, share) + lax.rem(feat + other, 2)
        slot = share * owner + lax.rem(rest, share)
        order = jnp.broadcast_to(rank_down, (k, k)) == slot.astype(F32)
        outs[3][...] = order.astype(F32).astype(BF)
        edge = iota((FEATS, k), 0)
        held = jnp.sum((jnp.broadcast_to(chosen, (FEATS, k)) < edge * feats).astype(F32), axis=1, keepdims=True)
        far = jnp.abs(held - (edge[:, :1] * share).astype(F32)) > share
        outs[4][...] = jnp.broadcast_to(jnp.max(far.astype(F32), axis=0, keepdims=True), outs[4].shape)
    for p in range(PARTS):
        cols = slice(p * wide, (p + 1) * wide)
        copies[p].wait()
        part = jnp.dot(hot_ref[...], buf_ref[:, cols], preferred_element_type=F32).astype(BF)
        if near:
            for i in range(3):
                outs[i][:, cols] = part[i * share : (i + 1) * share]
        else:
            outs[0][:, cols] = part


def pick(chosen, dec, near):
    feats, width = dec.shape
    k = chosen.shape[1]
    share = k // FEATS
    n = 3 * share if near else k
    if near:
        shapes = [(share, width)] * 3 + [(k, k), (8, 128), (share, width)]
        shapes = [jax.ShapeDtypeStruct(shape, F32 if shape[0] == 8 else BF) for shape in shapes]
        shapes[-1] = pltpu.HBM((share, width), BF)
        spaces = [pltpu.VMEM] * 5 + [pltpu.HBM]
    else:
        shapes, spaces = [jax.ShapeDtypeStruct((k, width), BF)], [pltpu.VMEM]
    return pl.pallas_call(
        lambda *refs: pick_kernel(near, *refs),
        in_specs=[pl.BlockSpec(memory_space=pltpu.HBM)] * 2,
        out_specs=[pl.BlockSpec(memory_space=space) for space in spaces],
        out_shape=shapes,
        scratch_shapes=[
            pltpu.VMEM((n, feats), BF),
            pltpu.VMEM((feats, width), BF),
            pltpu.VMEM((1, k), I32),
            pltpu.SemaphoreType.DMA((PARTS + 1,)),
        ],
        compiler_params=pltpu.CompilerParams(vmem_limit_bytes=12 * MIB),
        cost_estimate=pl.CostEstimate(flops=2 * n * feats * width, bytes_accessed=2 * feats * width, transcendentals=0),
        name="pick_near" if near else "pick_all",
    )(chosen, dec)


def after(up, down, room):
    return pl.pallas_call(
        lambda up_ref, down_ref, room_ref, out_ref: None,
        in_specs=[pl.BlockSpec(memory_space=pltpu.VMEM)] * 2 + [pl.BlockSpec(memory_space=pltpu.HBM)],
        out_specs=pl.BlockSpec(memory_space=pltpu.HBM),
        out_shape=pltpu.HBM(room.shape, room.dtype),
        input_output_aliases={2: 0},
        compiler_params=pltpu.CompilerParams(vmem_limit_bytes=MIB),
        name="after",
    )(up, down, pltpu.with_memory_space_constraint(room, pltpu.HBM))


def settle_kernel(own_ref, up_ref, down_ref, far_ref, room_ref, out_ref, sem):
    far = far_ref[0, 0] > 0.0

    @pl.when(far)
    def _():
        copy = pltpu.make_async_copy(room_ref, out_ref, sem)
        copy.start()
        copy.wait()

    @pl.when(jnp.logical_not(far))
    def _():
        out_ref[...] = own_ref[...] + up_ref[...] + down_ref[...]


def settle(own, up, down, far, room):
    return pl.pallas_call(
        settle_kernel,
        in_specs=[pl.BlockSpec(memory_space=pltpu.VMEM)] * 4 + [pl.BlockSpec(memory_space=pltpu.HBM)],
        out_specs=pl.BlockSpec(memory_space=pltpu.VMEM),
        out_shape=jax.ShapeDtypeStruct(own.shape, own.dtype),
        scratch_shapes=[pltpu.SemaphoreType.DMA],
        compiler_params=pltpu.CompilerParams(vmem_limit_bytes=2 * MIB),
        cost_estimate=pl.CostEstimate(flops=2 * own.size, bytes_accessed=8 * own.size, transcendentals=0),
        name="settle",
    )(own, up, down, far, room)


def fetch_kernel(own_ref, enc_ref, out_ref, same_ref, sem):
    copy = pltpu.make_async_copy(enc_ref, out_ref, sem)
    copy.start()
    same_ref[...] = own_ref[...]
    copy.wait()


def fetch(own, enc):
    return pl.pallas_call(
        fetch_kernel,
        in_specs=[pl.BlockSpec(memory_space=pltpu.VMEM), pl.BlockSpec(memory_space=pltpu.HBM)],
        out_specs=[pl.BlockSpec(memory_space=pltpu.VMEM)] * 2,
        out_shape=[pltpu.VMEM(enc.shape, enc.dtype), jax.ShapeDtypeStruct(own.shape, own.dtype)],
        scratch_shapes=[pltpu.SemaphoreType.DMA],
        compiler_params=pltpu.CompilerParams(vmem_limit_bytes=8 * MIB),
        cost_estimate=pl.CostEstimate(flops=0, bytes_accessed=4 * enc.size, transcendentals=0),
        name="fetch",
    )(own, enc)


def product_kernel(last, left_ref, enc_ref, *refs):
    half = left_ref.shape[0]
    if last:
        first_ref, order_ref, out_ref, rows_ref = refs
        rows_ref[:half, :] = first_ref[...]
    else:
        out_ref = rows_ref = refs[0]
    at = half if last else 0
    tile = 256
    for j in range(out_ref.shape[1] // tile):
        cols = slice(j * tile, (j + 1) * tile)
        part = jnp.dot(left_ref[...], enc_ref[:, cols], preferred_element_type=F32)
        rows_ref[at : at + half, cols] = part.astype(BF)
    if last:
        for j in range(out_ref.shape[1] // tile):
            cols = slice(j * tile, (j + 1) * tile)
            part = jnp.dot(order_ref[...], rows_ref[:, cols], preferred_element_type=F32)
            out_ref[:, cols] = part.astype(BF)


def product(left, enc, *more):
    half, width = left.shape
    n = enc.shape[1]
    last = bool(more)
    return pl.pallas_call(
        lambda *refs: product_kernel(last, *refs),
        in_specs=[pl.BlockSpec(memory_space=pltpu.VMEM)] * (2 + len(more)),
        out_specs=pl.BlockSpec(memory_space=pltpu.VMEM),
        out_shape=jax.ShapeDtypeStruct((2 * half if last else half, n), BF),
        scratch_shapes=[pltpu.VMEM((2 * half, n), BF)] if last else [],
        compiler_params=pltpu.CompilerParams(vmem_limit_bytes=16 * MIB),
        cost_estimate=pl.CostEstimate(flops=2 * half * n * width, bytes_accessed=2 * width * n, transcendentals=0),
        name="product_last" if last else "product_own",
    )(left, enc, *more)


def local(encoder, decoder, chosen):
    enc = pltpu.with_memory_space_constraint(encoder[0], pltpu.HBM)
    dec = pltpu.with_memory_space_constraint(decoder[0], pltpu.HBM)
    k, feats = chosen.shape[0], dec.shape[0]
    share = k // FEATS
    listed = pltpu.with_memory_space_constraint(chosen.reshape(1, k), pltpu.HBM)
    feat, layer = lax.axis_index("feat"), lax.axis_index("layer")
    x, core = feat // 2, feat % 2
    y, z = layer // 8, layer % 8

    def feat_step(v, move):
        return lax.ppermute(v, "feat", [(i, move(i) % FEATS) for i in range(FEATS)])

    def along_x(v, d):
        return feat_step(v, lambda i: i ^ (2 * d))

    def along_z(v, d):
        return lax.ppermute(v, "layer", [(i, i ^ d) for i in range(LAYERS)])

    below, own, above, order, far, room = pick(listed, dec, True)
    up = feat_step(above, lambda i: i + 1)
    down = feat_step(below, lambda i: i - 1)

    def general(state):
        (rows,) = pick(listed, dec, False)

        def chunk(d):
            return lax.dynamic_slice_in_dim(rows, share * ((feat + d) % FEATS), share, 0)

        total = chunk(0)
        for d in range(1, FEATS):
            total = total + feat_step(chunk(d), lambda i: i + d)
        return jnp.zeros_like(state[0]), total

    edges = jnp.arange(1, FEATS)
    held = jnp.sum((chosen[:, None] < edges[None, :] * feats).astype(I32), axis=0)
    close = jnp.all(jnp.abs(held - edges * share) <= share)
    room = lax.while_loop(lambda state: state[0], general, (jnp.logical_not(close), after(up, down, room)))[1]
    total = settle(own, up, down, far, room).astype(F32)

    before = jnp.zeros_like(total)

    def join(arrivals, before, total):
        for lower, v in arrivals:
            v = v.astype(F32)
            before = before + jnp.where(lower, v, 0.0)
            total = total + v
        return before, total

    low = total.astype(BF)
    arrivals = [((z ^ d) < z, along_z(low, d)) for d in (1,)]
    before, total = join(arrivals, before, total)
    def crossed(v, dy, dz, first):
        pairs = []
        for layer in range(LAYERS):
            for f in range(FEATS):
                to = layer ^ dz if (f % 2 == 1) == first else layer ^ (8 * dy)
                pairs.append((layer * FEATS + f, to * FEATS + f))
        return lax.ppermute(v, ("layer", "feat"), pairs)

    ways = tuple(zip((2, 3, 1), (5, 7, 2)))
    pair = total
    low = pair.astype(BF)
    for dy, dz in ways:
        v = crossed(low, dy, dz, True).astype(F32)
        lower = jnp.where(core == 1, (z ^ dz) < z, (y ^ dy) < y)
        if dy == 2:
            masked = jnp.where(lower, v, 0.0)
        else:
            masked = masked + jnp.where(lower, v, 0.0)
        total = total + v
    before = before + masked
    prefix = before
    for dy, dz in ways:
        out = jnp.where(core == 1, total, masked + jnp.where(z < (z ^ dz), pair, 0.0))
        v = crossed(out.astype(BF), dy, dz, False).astype(F32)
        prefix = prefix + jnp.where((core == 0) | ((y ^ dy) < y), v, 0.0)
    prefix = prefix.astype(BF)

    pieces = [along_x(prefix, d) for d in (3, 2, 1)]
    near, prefix = fetch(prefix, enc)
    whole = jnp.zeros((k // 2, prefix.shape[1]), BF)
    for d, piece in zip((0,) + (3, 2, 1), [prefix] + pieces):
        whole = lax.dynamic_update_slice_in_dim(whole, piece, share * (x ^ d), 0)
    other = feat_step(whole, lambda i: i ^ 1)
    return product(other, near, product(whole, near), order)[None]


def solution(mesh):
    placed = (P("layer", None, "feat"), P("layer", "feat", None), P())
    return jax.shard_map(
        local, mesh=mesh, in_specs=placed, out_specs=P("layer", None, "feat"), check_vma=False
    )
```

```python
import jax
import jax.numpy as jnp
from jax import lax
from jax.experimental import pallas as pl
from jax.experimental.pallas import tpu as pltpu
from jax.sharding import PartitionSpec as P

BF = jnp.bfloat16
F32 = jnp.float32
I32 = jnp.int32
MIB = 2**20
PARTS = 6
FEATS = 8
LAYERS = 32


def iota(shape, axis):
    return lax.broadcasted_iota(I32, shape, axis)


def ranks_of(chosen):
    k = chosen.shape[1]
    along = jnp.broadcast_to(chosen, (k, k))
    down = along.T
    row, lane = iota((k, k), 0), iota((k, k), 1)
    b_first = (along < down) | ((along == down) & (lane < row))
    a_first = (down < along) | ((along == down) & (row < lane))
    rank_down = jnp.sum(b_first.astype(F32), axis=1, keepdims=True)
    rank_along = jnp.sum(a_first.astype(F32), axis=0, keepdims=True)
    return rank_down, rank_along


def slots_onehot(chosen, rank_along, first, n, base, hot_ref):
    k = chosen.shape[1]
    feats = hot_ref.shape[1]
    slot = (first + iota((n, k), 0)).astype(F32)
    here = jnp.broadcast_to(rank_along, (n, k)) == slot
    value = jnp.where(here, jnp.broadcast_to(chosen.astype(F32) + 1.0, (n, k)), 0.0)
    feature = jnp.sum(value, axis=1, keepdims=True) - 1.0 - base.astype(F32)
    feature = jnp.broadcast_to(feature, (n, k))
    lane = iota((n, k), 1).astype(F32)
    for j in range(feats // k):
        hot_ref[:, j * k : (j + 1) * k] = (feature == lane + float(j * k)).astype(F32).astype(BF)


def pick_kernel(near, chosen_ref, dec_ref, *refs):
    outs, (hot_ref, buf_ref, list_ref, sems) = refs[:-4], refs[-4:]
    n, feats = hot_ref.shape
    k = list_ref.shape[1]
    width = buf_ref.shape[1]
    wide = width // PARTS
    share = k // FEATS
    feat = lax.axis_index("feat")
    listed = pltpu.make_async_copy(chosen_ref, list_ref, sems.at[PARTS])
    listed.start()
    copies = []
    for p in range(PARTS):
        cols = pl.ds(p * wide, wide)
        copies.append(pltpu.make_async_copy(dec_ref.at[:, cols], buf_ref.at[:, cols], sems.at[p]))
        copies[p].start()
    listed.wait()
    chosen = list_ref[...]
    rank_down, rank_along = ranks_of(chosen)
    first = share * (feat - 1) if near else 0
    slots_onehot(chosen, rank_along, first, n, feat * feats, hot_ref)
    if near:
        p = iota((k, k), 1)
        half = k // 2
        other, rest = lax.div(p, half), lax.rem(p, half)
        owner = 2 * lax.div(rest, share) + lax.rem(feat + other, 2)
        slot = share * owner + lax.rem(rest, share)
        order = jnp.broadcast_to(rank_down, (k, k)) == slot.astype(F32)
        outs[3][...] = order.astype(F32).astype(BF)
        edge = iota((FEATS, k), 0)
        held = jnp.sum((jnp.broadcast_to(chosen, (FEATS, k)) < edge * feats).astype(F32), axis=1, keepdims=True)
        far = jnp.abs(held - (edge[:, :1] * share).astype(F32)) > share
        outs[4][...] = jnp.broadcast_to(jnp.max(far.astype(F32), axis=0, keepdims=True), outs[4].shape)
    for p in range(PARTS):
        cols = slice(p * wide, (p + 1) * wide)
        copies[p].wait()
        part = jnp.dot(hot_ref[...], buf_ref[:, cols], preferred_element_type=F32).astype(BF)
        if near:
            for i in range(3):
                outs[i][:, cols] = part[i * share : (i + 1) * share]
        else:
            outs[0][:, cols] = part


def pick(chosen, dec, near):
    feats, width = dec.shape
    k = chosen.shape[1]
    share = k // FEATS
    n = 3 * share if near else k
    if near:
        shapes = [(share, width)] * 3 + [(k, k), (8, 128), (share, width)]
        shapes = [jax.ShapeDtypeStruct(shape, F32 if shape[0] == 8 else BF) for shape in shapes]
        shapes[-1] = pltpu.HBM((share, width), BF)
        spaces = [pltpu.VMEM] * 5 + [pltpu.HBM]
    else:
        shapes, spaces = [jax.ShapeDtypeStruct((k, width), BF)], [pltpu.VMEM]
    return pl.pallas_call(
        lambda *refs: pick_kernel(near, *refs),
        in_specs=[pl.BlockSpec(memory_space=pltpu.HBM)] * 2,
        out_specs=[pl.BlockSpec(memory_space=space) for space in spaces],
        out_shape=shapes,
        scratch_shapes=[
            pltpu.VMEM((n, feats), BF),
            pltpu.VMEM((feats, width), BF),
            pltpu.VMEM((1, k), I32),
            pltpu.SemaphoreType.DMA((PARTS + 1,)),
        ],
        compiler_params=pltpu.CompilerParams(vmem_limit_bytes=12 * MIB),
        cost_estimate=pl.CostEstimate(flops=2 * n * feats * width, bytes_accessed=2 * feats * width, transcendentals=0),
        name="pick_near" if near else "pick_all",
    )(chosen, dec)


def after(up, down, room):
    return pl.pallas_call(
        lambda up_ref, down_ref, room_ref, out_ref: None,
        in_specs=[pl.BlockSpec(memory_space=pltpu.VMEM)] * 2 + [pl.BlockSpec(memory_space=pltpu.HBM)],
        out_specs=pl.BlockSpec(memory_space=pltpu.HBM),
        out_shape=pltpu.HBM(room.shape, room.dtype),
        input_output_aliases={2: 0},
        compiler_params=pltpu.CompilerParams(vmem_limit_bytes=MIB),
        name="after",
    )(up, down, pltpu.with_memory_space_constraint(room, pltpu.HBM))


def settle_kernel(own_ref, up_ref, down_ref, far_ref, room_ref, out_ref, sem):
    far = far_ref[0, 0] > 0.0

    @pl.when(far)
    def _():
        copy = pltpu.make_async_copy(room_ref, out_ref, sem)
        copy.start()
        copy.wait()

    @pl.when(jnp.logical_not(far))
    def _():
        out_ref[...] = own_ref[...] + up_ref[...] + down_ref[...]


def settle(own, up, down, far, room):
    return pl.pallas_call(
        settle_kernel,
        in_specs=[pl.BlockSpec(memory_space=pltpu.VMEM)] * 4 + [pl.BlockSpec(memory_space=pltpu.HBM)],
        out_specs=pl.BlockSpec(memory_space=pltpu.VMEM),
        out_shape=jax.ShapeDtypeStruct(own.shape, own.dtype),
        scratch_shapes=[pltpu.SemaphoreType.DMA],
        compiler_params=pltpu.CompilerParams(vmem_limit_bytes=2 * MIB),
        cost_estimate=pl.CostEstimate(flops=2 * own.size, bytes_accessed=8 * own.size, transcendentals=0),
        name="settle",
    )(own, up, down, far, room)


def fetch_kernel(own_ref, enc_ref, out_ref, same_ref, sem):
    copy = pltpu.make_async_copy(enc_ref, out_ref, sem)
    copy.start()
    same_ref[...] = own_ref[...]
    copy.wait()


def fetch(own, enc):
    return pl.pallas_call(
        fetch_kernel,
        in_specs=[pl.BlockSpec(memory_space=pltpu.VMEM), pl.BlockSpec(memory_space=pltpu.HBM)],
        out_specs=[pl.BlockSpec(memory_space=pltpu.VMEM)] * 2,
        out_shape=[pltpu.VMEM(enc.shape, enc.dtype), jax.ShapeDtypeStruct(own.shape, own.dtype)],
        scratch_shapes=[pltpu.SemaphoreType.DMA],
        compiler_params=pltpu.CompilerParams(vmem_limit_bytes=8 * MIB),
        cost_estimate=pl.CostEstimate(flops=0, bytes_accessed=4 * enc.size, transcendentals=0),
        name="fetch",
    )(own, enc)


def product_kernel(last, left_ref, enc_ref, *refs):
    half = left_ref.shape[0]
    if last:
        first_ref, order_ref, out_ref, rows_ref = refs
        rows_ref[:half, :] = first_ref[...]
    else:
        out_ref = rows_ref = refs[0]
    at = half if last else 0
    tile = 256
    for j in range(out_ref.shape[1] // tile):
        cols = slice(j * tile, (j + 1) * tile)
        part = jnp.dot(left_ref[...], enc_ref[:, cols], preferred_element_type=F32)
        rows_ref[at : at + half, cols] = part.astype(BF)
    if last:
        for j in range(out_ref.shape[1] // tile):
            cols = slice(j * tile, (j + 1) * tile)
            part = jnp.dot(order_ref[...], rows_ref[:, cols], preferred_element_type=F32)
            out_ref[:, cols] = part.astype(BF)


def product(left, enc, *more):
    half, width = left.shape
    n = enc.shape[1]
    last = bool(more)
    return pl.pallas_call(
        lambda *refs: product_kernel(last, *refs),
        in_specs=[pl.BlockSpec(memory_space=pltpu.VMEM)] * (2 + len(more)),
        out_specs=pl.BlockSpec(memory_space=pltpu.VMEM),
        out_shape=jax.ShapeDtypeStruct((2 * half if last else half, n), BF),
        scratch_shapes=[pltpu.VMEM((2 * half, n), BF)] if last else [],
        compiler_params=pltpu.CompilerParams(vmem_limit_bytes=16 * MIB),
        cost_estimate=pl.CostEstimate(flops=2 * half * n * width, bytes_accessed=2 * width * n, transcendentals=0),
        name="product_last" if last else "product_own",
    )(left, enc, *more)


def local(encoder, decoder, chosen):
    enc = pltpu.with_memory_space_constraint(encoder[0], pltpu.HBM)
    dec = pltpu.with_memory_space_constraint(decoder[0], pltpu.HBM)
    k, feats = chosen.shape[0], dec.shape[0]
    share = k // FEATS
    listed = pltpu.with_memory_space_constraint(chosen.reshape(1, k), pltpu.HBM)
    feat, layer = lax.axis_index("feat"), lax.axis_index("layer")
    x, core = feat // 2, feat % 2
    y, z = layer // 8, layer % 8

    def feat_step(v, move):
        return lax.ppermute(v, "feat", [(i, move(i) % FEATS) for i in range(FEATS)])

    def along_x(v, d):
        return feat_step(v, lambda i: i ^ (2 * d))

    def along_z(v, d):
        return lax.ppermute(v, "layer", [(i, i ^ d) for i in range(LAYERS)])

    below, own, above, order, far, room = pick(listed, dec, True)
    up = feat_step(above, lambda i: i + 1)
    down = feat_step(below, lambda i: i - 1)

    def general(state):
        (rows,) = pick(listed, dec, False)

        def chunk(d):
            return lax.dynamic_slice_in_dim(rows, share * ((feat + d) % FEATS), share, 0)

        total = chunk(0)
        for d in range(1, FEATS):
            total = total + feat_step(chunk(d), lambda i: i + d)
        return jnp.zeros_like(state[0]), total

    edges = jnp.arange(1, FEATS)
    held = jnp.sum((chosen[:, None] < edges[None, :] * feats).astype(I32), axis=0)
    close = jnp.all(jnp.abs(held - edges * share) <= share)
    room = lax.while_loop(lambda state: state[0], general, (jnp.logical_not(close), after(up, down, room)))[1]
    total = settle(own, up, down, far, room).astype(F32)

    before = jnp.zeros_like(total)

    def join(arrivals, before, total):
        for lower, v in arrivals:
            v = v.astype(F32)
            before = before + jnp.where(lower, v, 0.0)
            total = total + v
        return before, total

    low = total.astype(BF)
    arrivals = [((z ^ d) < z, along_z(low, d)) for d in (1,)]
    before, total = join(arrivals, before, total)
    def crossed(v, dy, dz, first):
        pairs = []
        for layer in range(LAYERS):
            for f in range(FEATS):
                to = layer ^ dz if (f % 2 == 1) == first else layer ^ (8 * dy)
                pairs.append((layer * FEATS + f, to * FEATS + f))
        return lax.ppermute(v, ("layer", "feat"), pairs)

    ways = ((2, 5), (3, 7), (1, 2))
    pair = total
    low = pair.astype(BF)
    for dy, dz in ways:
        v = crossed(low, dy, dz, True).astype(F32)
        lower = jnp.where(core == 1, (z ^ dz) < z, (y ^ dy) < y)
        if dy == 2:
            masked = jnp.where(lower, v, 0.0)
        else:
            masked = masked + jnp.where(lower, v, 0.0)
        total = total + v
    before = before + masked
    prefix = before
    for dy, dz in ((3, 5), (2, 7), (1, 2)):
        out = jnp.where(core == 1, total, masked + jnp.where(z < (z ^ dz), pair, 0.0))
        v = crossed(out.astype(BF), dy, dz, False).astype(F32)
        prefix = prefix + jnp.where((core == 0) | ((y ^ dy) < y), v, 0.0)
    prefix = prefix.astype(BF)

    pieces = [along_x(prefix, d) for d in (3, 2, 1)]
    near, prefix = fetch(prefix, enc)
    whole = jnp.zeros((k // 2, prefix.shape[1]), BF)
    for d, piece in zip((0,) + (3, 2, 1), [prefix] + pieces):
        whole = lax.dynamic_update_slice_in_dim(whole, piece, share * (x ^ d), 0)
    other = feat_step(whole, lambda i: i ^ 1)
    return product(other, near, product(whole, near), order)[None]


def solution(mesh):
    placed = (P("layer", None, "feat"), P("layer", "feat", None), P())
    return jax.shard_map(
        local, mesh=mesh, in_specs=placed, out_specs=P("layer", None, "feat"), check_vma=False
    )
```

```python
import jax
import jax.numpy as jnp
from jax import lax
from jax.experimental import pallas as pl
from jax.experimental.pallas import tpu as pltpu
from jax.sharding import PartitionSpec as P

BF = jnp.bfloat16
F32 = jnp.float32
I32 = jnp.int32
MIB = 2**20
PARTS = 6
FEATS = 8
LAYERS = 32


def iota(shape, axis):
    return lax.broadcasted_iota(I32, shape, axis)


def ranks_of(chosen):
    k = chosen.shape[1]
    along = jnp.broadcast_to(chosen, (k, k))
    down = along.T
    row, lane = iota((k, k), 0), iota((k, k), 1)
    b_first = (along < down) | ((along == down) & (lane < row))
    a_first = (down < along) | ((along == down) & (row < lane))
    rank_down = jnp.sum(b_first.astype(F32), axis=1, keepdims=True)
    rank_along = jnp.sum(a_first.astype(F32), axis=0, keepdims=True)
    return rank_down, rank_along


def slots_onehot(chosen, rank_along, first, n, base, hot_ref):
    k = chosen.shape[1]
    feats = hot_ref.shape[1]
    slot = (first + iota((n, k), 0)).astype(F32)
    here = jnp.broadcast_to(rank_along, (n, k)) == slot
    value = jnp.where(here, jnp.broadcast_to(chosen.astype(F32) + 1.0, (n, k)), 0.0)
    feature = jnp.sum(value, axis=1, keepdims=True) - 1.0 - base.astype(F32)
    feature = jnp.broadcast_to(feature, (n, k))
    lane = iota((n, k), 1).astype(F32)
    for j in range(feats // k):
        hot_ref[:, j * k : (j + 1) * k] = (feature == lane + float(j * k)).astype(F32).astype(BF)


def pick_kernel(near, chosen_ref, dec_ref, *refs):
    outs, (hot_ref, buf_ref, list_ref, sems) = refs[:-4], refs[-4:]
    n, feats = hot_ref.shape
    k = list_ref.shape[1]
    width = buf_ref.shape[1]
    wide = width // PARTS
    share = k // FEATS
    feat = lax.axis_index("feat")
    listed = pltpu.make_async_copy(chosen_ref, list_ref, sems.at[PARTS])
    listed.start()
    copies = []
    for p in range(PARTS):
        cols = pl.ds(p * wide, wide)
        copies.append(pltpu.make_async_copy(dec_ref.at[:, cols], buf_ref.at[:, cols], sems.at[p]))
        copies[p].start()
    listed.wait()
    chosen = list_ref[...]
    rank_down, rank_along = ranks_of(chosen)
    first = share * (feat - 1) if near else 0
    slots_onehot(chosen, rank_along, first, n, feat * feats, hot_ref)
    if near:
        p = iota((k, k), 1)
        half = k // 2
        other, rest = lax.div(p, half), lax.rem(p, half)
        owner = 2 * lax.div(rest, share) + lax.rem(feat + other, 2)
        slot = share * owner + lax.rem(rest, share)
        order = jnp.broadcast_to(rank_down, (k, k)) == slot.astype(F32)
        outs[3][...] = order.astype(F32).astype(BF)
        edge = iota((FEATS, k), 0)
        held = jnp.sum((jnp.broadcast_to(chosen, (FEATS, k)) < edge * feats).astype(F32), axis=1, keepdims=True)
        far = jnp.abs(held - (edge[:, :1] * share).astype(F32)) > share
        outs[4][...] = jnp.broadcast_to(jnp.max(far.astype(F32), axis=0, keepdims=True), outs[4].shape)
    for p in range(PARTS):
        cols = slice(p * wide, (p + 1) * wide)
        copies[p].wait()
        part = jnp.dot(hot_ref[...], buf_ref[:, cols], preferred_element_type=F32).astype(BF)
        if near:
            for i in range(3):
                outs[i][:, cols] = part[i * share : (i + 1) * share]
        else:
            outs[0][:, cols] = part


def pick(chosen, dec, near):
    feats, width = dec.shape
    k = chosen.shape[1]
    share = k // FEATS
    n = 3 * share if near else k
    if near:
        shapes = [(share, width)] * 3 + [(k, k), (8, 128), (share, width)]
        shapes = [jax.ShapeDtypeStruct(shape, F32 if shape[0] == 8 else BF) for shape in shapes]
        shapes[-1] = pltpu.HBM((share, width), BF)
        spaces = [pltpu.VMEM] * 5 + [pltpu.HBM]
    else:
        shapes, spaces = [jax.ShapeDtypeStruct((k, width), BF)], [pltpu.VMEM]
    return pl.pallas_call(
        lambda *refs: pick_kernel(near, *refs),
        in_specs=[pl.BlockSpec(memory_space=pltpu.HBM)] * 2,
        out_specs=[pl.BlockSpec(memory_space=space) for space in spaces],
        out_shape=shapes,
        scratch_shapes=[
            pltpu.VMEM((n, feats), BF),
            pltpu.VMEM((feats, width), BF),
            pltpu.VMEM((1, k), I32),
            pltpu.SemaphoreType.DMA((PARTS + 1,)),
        ],
        compiler_params=pltpu.CompilerParams(vmem_limit_bytes=12 * MIB),
        cost_estimate=pl.CostEstimate(flops=2 * n * feats * width, bytes_accessed=2 * feats * width, transcendentals=0),
        name="pick_near" if near else "pick_all",
    )(chosen, dec)


def after(up, down, room):
    return pl.pallas_call(
        lambda up_ref, down_ref, room_ref, out_ref: None,
        in_specs=[pl.BlockSpec(memory_space=pltpu.VMEM)] * 2 + [pl.BlockSpec(memory_space=pltpu.HBM)],
        out_specs=pl.BlockSpec(memory_space=pltpu.HBM),
        out_shape=pltpu.HBM(room.shape, room.dtype),
        input_output_aliases={2: 0},
        compiler_params=pltpu.CompilerParams(vmem_limit_bytes=MIB),
        name="after",
    )(up, down, pltpu.with_memory_space_constraint(room, pltpu.HBM))


def settle_kernel(own_ref, up_ref, down_ref, far_ref, room_ref, out_ref, sem):
    far = far_ref[0, 0] > 0.0

    @pl.when(far)
    def _():
        copy = pltpu.make_async_copy(room_ref, out_ref, sem)
        copy.start()
        copy.wait()

    @pl.when(jnp.logical_not(far))
    def _():
        out_ref[...] = own_ref[...] + up_ref[...] + down_ref[...]


def settle(own, up, down, far, room):
    return pl.pallas_call(
        settle_kernel,
        in_specs=[pl.BlockSpec(memory_space=pltpu.VMEM)] * 4 + [pl.BlockSpec(memory_space=pltpu.HBM)],
        out_specs=pl.BlockSpec(memory_space=pltpu.VMEM),
        out_shape=jax.ShapeDtypeStruct(own.shape, own.dtype),
        scratch_shapes=[pltpu.SemaphoreType.DMA],
        compiler_params=pltpu.CompilerParams(vmem_limit_bytes=2 * MIB),
        cost_estimate=pl.CostEstimate(flops=2 * own.size, bytes_accessed=8 * own.size, transcendentals=0),
        name="settle",
    )(own, up, down, far, room)


def fetch_kernel(own_ref, enc_ref, out_ref, same_ref, sem):
    copy = pltpu.make_async_copy(enc_ref, out_ref, sem)
    copy.start()
    same_ref[...] = own_ref[...]
    copy.wait()


def fetch(own, enc):
    return pl.pallas_call(
        fetch_kernel,
        in_specs=[pl.BlockSpec(memory_space=pltpu.VMEM), pl.BlockSpec(memory_space=pltpu.HBM)],
        out_specs=[pl.BlockSpec(memory_space=pltpu.VMEM)] * 2,
        out_shape=[pltpu.VMEM(enc.shape, enc.dtype), jax.ShapeDtypeStruct(own.shape, own.dtype)],
        scratch_shapes=[pltpu.SemaphoreType.DMA],
        compiler_params=pltpu.CompilerParams(vmem_limit_bytes=8 * MIB),
        cost_estimate=pl.CostEstimate(flops=0, bytes_accessed=4 * enc.size, transcendentals=0),
        name="fetch",
    )(own, enc)


def product_kernel(last, left_ref, enc_ref, *refs):
    half = left_ref.shape[0]
    if last:
        first_ref, order_ref, out_ref, rows_ref = refs
        rows_ref[:half, :] = first_ref[...]
    else:
        out_ref = rows_ref = refs[0]
    at = half if last else 0
    tile = 256
    for j in range(out_ref.shape[1] // tile):
        cols = slice(j * tile, (j + 1) * tile)
        part = jnp.dot(left_ref[...], enc_ref[:, cols], preferred_element_type=F32)
        rows_ref[at : at + half, cols] = part.astype(BF)
    if last:
        for j in range(out_ref.shape[1] // tile):
            cols = slice(j * tile, (j + 1) * tile)
            part = jnp.dot(order_ref[...], rows_ref[:, cols], preferred_element_type=F32)
            out_ref[:, cols] = part.astype(BF)


def product(left, enc, *more):
    half, width = left.shape
    n = enc.shape[1]
    last = bool(more)
    return pl.pallas_call(
        lambda *refs: product_kernel(last, *refs),
        in_specs=[pl.BlockSpec(memory_space=pltpu.VMEM)] * (2 + len(more)),
        out_specs=pl.BlockSpec(memory_space=pltpu.VMEM),
        out_shape=jax.ShapeDtypeStruct((2 * half if last else half, n), BF),
        scratch_shapes=[pltpu.VMEM((2 * half, n), BF)] if last else [],
        compiler_params=pltpu.CompilerParams(vmem_limit_bytes=16 * MIB),
        cost_estimate=pl.CostEstimate(flops=2 * half * n * width, bytes_accessed=2 * width * n, transcendentals=0),
        name="product_last" if last else "product_own",
    )(left, enc, *more)


def local(encoder, decoder, chosen):
    enc = pltpu.with_memory_space_constraint(encoder[0], pltpu.HBM)
    dec = pltpu.with_memory_space_constraint(decoder[0], pltpu.HBM)
    k, feats = chosen.shape[0], dec.shape[0]
    share = k // FEATS
    listed = pltpu.with_memory_space_constraint(chosen.reshape(1, k), pltpu.HBM)
    feat, layer = lax.axis_index("feat"), lax.axis_index("layer")
    x, core = feat // 2, feat % 2
    y, z = layer // 8, layer % 8

    def feat_step(v, move):
        return lax.ppermute(v, "feat", [(i, move(i) % FEATS) for i in range(FEATS)])

    def along_x(v, d):
        return feat_step(v, lambda i: i ^ (2 * d))

    def along_z(v, d):
        return lax.ppermute(v, "layer", [(i, i ^ d) for i in range(LAYERS)])

    below, own, above, order, far, room = pick(listed, dec, True)
    up = feat_step(above, lambda i: i + 1)
    down = feat_step(below, lambda i: i - 1)

    def general(state):
        (rows,) = pick(listed, dec, False)

        def chunk(d):
            return lax.dynamic_slice_in_dim(rows, share * ((feat + d) % FEATS), share, 0)

        total = chunk(0)
        for d in range(1, FEATS):
            total = total + feat_step(chunk(d), lambda i: i + d)
        return jnp.zeros_like(state[0]), total

    edges = jnp.arange(1, FEATS)
    held = jnp.sum((chosen[:, None] < edges[None, :] * feats).astype(I32), axis=0)
    close = jnp.all(jnp.abs(held - edges * share) <= share)
    room = lax.while_loop(lambda state: state[0], general, (jnp.logical_not(close), after(up, down, room)))[1]
    total = settle(own, up, down, far, room).astype(F32)

    before = jnp.zeros_like(total)

    def join(arrivals, before, total):
        for lower, v in arrivals:
            v = v.astype(F32)
            before = before + jnp.where(lower, v, 0.0)
            total = total + v
        return before, total

    low = total.astype(BF)
    arrivals = [((z ^ d) < z, along_z(low, d)) for d in (1,)]
    before, total = join(arrivals, before, total)
    def crossed(v, dy, dz, first):
        pairs = []
        for layer in range(LAYERS):
            for f in range(FEATS):
                to = layer ^ dz if (f % 2 == 1) == first else layer ^ (8 * dy)
                pairs.append((layer * FEATS + f, to * FEATS + f))
        return lax.ppermute(v, ("layer", "feat"), pairs)

    ways = ((2, 5), (3, 2), (1, 7))
    pair = total
    low = pair.astype(BF)
    for dy, dz in ways:
        v = crossed(low, dy, dz, True).astype(F32)
        lower = jnp.where(core == 1, (z ^ dz) < z, (y ^ dy) < y)
        if dy == 2:
            masked = jnp.where(lower, v, 0.0)
        else:
            masked = masked + jnp.where(lower, v, 0.0)
        total = total + v
    before = before + masked
    prefix = before
    for dy, dz in ((3, 5), (2, 7), (1, 2)):
        out = jnp.where(core == 1, total, masked + jnp.where(z < (z ^ dz), pair, 0.0))
        v = crossed(out.astype(BF), dy, dz, False).astype(F32)
        prefix = prefix + jnp.where((core == 0) | ((y ^ dy) < y), v, 0.0)
    prefix = prefix.astype(BF)

    pieces = [along_x(prefix, d) for d in (3, 2, 1)]
    near, prefix = fetch(prefix, enc)
    whole = jnp.zeros((k // 2, prefix.shape[1]), BF)
    for d, piece in zip((0,) + (3, 2, 1), [prefix] + pieces):
        whole = lax.dynamic_update_slice_in_dim(whole, piece, share * (x ^ d), 0)
    other = feat_step(whole, lambda i: i ^ 1)
    return product(other, near, product(whole, near), order)[None]


def solution(mesh):
    placed = (P("layer", None, "feat"), P("layer", "feat", None), P())
    return jax.shard_map(
        local, mesh=mesh, in_specs=placed, out_specs=P("layer", None, "feat"), check_vma=False
    )
```
